256 devices in a mesh: row: 8 (over z), col: 32 (over y, x, core).
Axes of the slice: x: 4, y: 4, z: 8, core: 2. Of those that a mesh axis runs over, the one named last changes fastest.
Arguments:
- p_vals: float32 [256, 12, 128, 128], P(('row', 'col')), may hold values from -1.5 to 1.5
- p_cols: int32 [256, 12], replicated, may hold values from 0 to 255, as said below
- perm: int32 [256], replicated, may hold values from 0 to 255, as said below
- out_pattern: int32 [8, 32, 24, 2], P('row', 'col'), may hold values from 0 to 255, as said below
- branch_flag: int32 [8, 32], P('row', 'col'), may hold values 0 or 1
Outputs:
- next_blocks: float32 [8, 32, 24, 128, 128], P('row', 'col')
The draws below stay inside these ranges and needn't reach their ends.
Inputs may be any that keep to these rules, and one draw needn't show every extreme that they name: `p_cols`: the 12 block columns of each stored row are distinct. `perm`: A permutation. The row stored at position r * 32 + c (grid row r, grid column c) has an index whose quotient by 8 is c. `out_pattern`: in tile (r, c) each first index is the row stored at position r * 32 + ((c + d) mod 32) for some d with -3 <= d <= 3, and every tile has entries with d = -3 and with d = 3; each second index is a row stored in grid column c; the 24 pairs of a tile are distinct.
All inputs are finite; a program needn't handle non-finite values. No bound on the sum of `branch_flag` on one device may be relied on, other than what follows from the above.
Results may differ from the reference program's by a relative error of at most 0.0003.
Values sent between devices are 32-bit elements; how exact they have to be, the bound alone decides.
No kernel may reach another device: no remote copies, remote signals or barrier semaphores. Data moves between devices by JAX's collectives and lax.ppermute only.
A program may use at most 64 MiB of HBM per device.

```python
import jax
import jax.numpy as jnp
from jax import lax

BS = 128
NNZ = 12
WG = 3
OT = 24
ROW_GROUPS = 8
COLUMN_GROUPS = 32
BLOCK_ROWS = 256


def shared_layout(key):
    layout_key = jax.random.fold_in(key, 11)
    group_keys = jax.random.split(layout_key, COLUMN_GROUPS)
    orders = jax.vmap(lambda subkey: jax.random.permutation(subkey, ROW_GROUPS))(group_keys).astype(jnp.int32)
    group_ids = jnp.arange(COLUMN_GROUPS, dtype=jnp.int32)
    stored = group_ids[None, :] * ROW_GROUPS + orders.T
    return stored.reshape(-1)


def draw_perm(key, part):
    return shared_layout(key)


def draw_p_cols(key, part):
    stored = shared_layout(key)
    key = jax.random.fold_in(key, 3)
    row_total = ROW_GROUPS * COLUMN_GROUPS
    row_keys = jax.random.split(key, row_total)
    offsets = jax.vmap(lambda subkey: jax.random.permutation(subkey, 32)[:NNZ])(row_keys).astype(jnp.int32)
    row_ids = jnp.arange(row_total, dtype=jnp.int32)
    by_row = jnp.mod(row_ids[:, None] + offsets - 16, row_total)
    return by_row[stored].astype(jnp.int32)


def draw_out_pattern(key, part):
    stored = shared_layout(key)
    key = jax.random.fold_in(key, 5)
    band_width = 2 * WG + 1
    candidates = band_width * ROW_GROUPS
    tile_count = ROW_GROUPS * COLUMN_GROUPS
    score_key, extreme_key, shuffle_key = jax.random.split(key, 3)
    scores = jax.random.randint(score_key, (tile_count, candidates), 0, 1 << 20) * candidates + jnp.arange(candidates)
    extremes = jax.random.randint(extreme_key, (tile_count, 2), 0, ROW_GROUPS)
    first_slot = extremes[:, 0]
    last_slot = (band_width - 1) * ROW_GROUPS + extremes[:, 1]
    slot_ids = jnp.arange(candidates)[None, :]
    scores = jnp.where(slot_ids == first_slot[:, None], -2, scores)
    scores = jnp.where(slot_ids == last_slot[:, None], -1, scores)
    chosen = jnp.argsort(scores, axis=1)[:, :OT]
    shuffle = jax.vmap(lambda subkey: jax.random.permutation(subkey, OT))(jax.random.split(shuffle_key, tile_count))
    chosen = jnp.take_along_axis(chosen, shuffle, axis=1)
    offset = chosen // ROW_GROUPS - WG
    grid_row = chosen % ROW_GROUPS
    tile_ids = jnp.arange(tile_count)
    tile_row = tile_ids // COLUMN_GROUPS
    tile_col = tile_ids % COLUMN_GROUPS
    row_pos = tile_row[:, None] * COLUMN_GROUPS + jnp.mod(tile_col[:, None] + offset, COLUMN_GROUPS)
    col_pos = grid_row * COLUMN_GROUPS + tile_col[:, None]
    out_pairs = jnp.stack([stored[row_pos], stored[col_pos]], axis=-1)
    return out_pairs.reshape(ROW_GROUPS, COLUMN_GROUPS, OT, 2).astype(jnp.int32)


def plant(drawn, key, smallest, largest):
    longest = drawn.shape.index(max(drawn.shape))
    spots = []
    for shift in (0, 1):
        where = [jax.random.randint(jax.random.fold_in(key, axis), (), 0, length) for axis, length in enumerate(drawn.shape)]
        where[longest] = (where[longest] + shift) % drawn.shape[longest]
        spots.append(tuple(where))
    return drawn.at[spots[0]].set(smallest).at[spots[1]].set(largest)


def steps_of(rng, extent, cuts, smallest, high):
    factor_of, own = 1.0, jax.random.fold_in(rng, 6)
    for dim, shards_of in cuts:
        draws = jnp.exp(jax.random.uniform(jax.random.fold_in(own, dim), (shards_of,), jnp.float32, smallest / len(cuts), high / len(cuts)))
        factor_of = factor_of * jnp.repeat(draws, extent[dim] // shards_of).reshape([-1 if axis == dim else 1 for axis in range(len(extent))])
    return factor_of


def centred(key, extent, deviation, reach, pieces=(), kind=jnp.bfloat16):
    entries = jax.random.normal(key, extent, jnp.float32) * deviation
    if len(pieces) > 0:
        entries = steps_of(key, extent, pieces, -0.22, 0.18) * entries
    return jnp.clip(entries, min=-reach, max=reach).astype(kind)


def setup_inputs(seed: int = 0) -> dict:
    keys = jax.random.split(jax.random.key(seed), 6)
    p_vals = centred(keys[0], (BLOCK_ROWS, NNZ, BS, BS), 0.25, 1.5, ((0, 256),), jnp.float32)
    p_cols = draw_p_cols(jax.random.fold_in(keys[5], 71), 0)
    perm = draw_perm(jax.random.fold_in(keys[5], 71), 0)
    out_pattern = draw_out_pattern(jax.random.fold_in(keys[5], 71), 0)
    branch_flag = plant((jax.random.randint(keys[4], (ROW_GROUPS, COLUMN_GROUPS), 0, 2) < 1).astype(jnp.int32), jax.random.fold_in(keys[4], 1), 0, 1)
    return dict(p_vals=p_vals, p_cols=p_cols, perm=perm, out_pattern=out_pattern, branch_flag=branch_flag)


def reference(p_vals, p_cols, perm, out_pattern, branch_flag):
    row_total = perm.shape[0]
    where_stored = jnp.zeros((row_total,), jnp.int32).at[perm].set(jnp.arange(row_total, dtype=jnp.int32))
    out_pairs = out_pattern.reshape((-1, 2))
    tile_flags = jnp.broadcast_to(branch_flag[:, :, None], out_pattern.shape[:3]).reshape((-1,))

    def one_block(items):
        out_pair, flag_value = items
        left_pos = where_stored[out_pair[0]]
        right_pos = where_stored[out_pair[1]]
        left_blocks = p_vals[left_pos]
        right_blocks = p_vals[right_pos]
        left_cols = p_cols[left_pos]
        right_cols = p_cols[right_pos]
        matches = (left_cols[:, None] == right_cols[None, :]).astype(left_blocks.dtype)
        chosen = jnp.einsum("st,tyk->syk", matches, right_blocks, precision=lax.Precision.HIGHEST)
        square = jnp.einsum("sxk,syk->xy", left_blocks, chosen, precision=lax.Precision.HIGHEST)
        hit_mask = (left_cols == out_pair[1]).astype(left_blocks.dtype)
        own_block = jnp.einsum("s,sxy->xy", hit_mask, left_blocks, precision=lax.Precision.HIGHEST)
        return jnp.where(flag_value == 1, 2.0 * own_block - square, square)

    blocks = lax.map(one_block, (out_pairs, tile_flags))
    return blocks.reshape(out_pattern.shape[:3] + (BS, BS))
```

```python
import functools

import jax
import jax.numpy as jnp
from jax import lax
from jax.experimental import pallas as pl
from jax.experimental.pallas import tpu as pltpu
from jax.sharding import PartitionSpec as P

BS = 128
NNZ = 12
OT = 24
HALF = NNZ // 2
UNROLL = 4
LIST = 320
Z_STEPS = (0, -1, 1, -2, 2, -3, 3, 4)
X_EVEN = (0, 1, 2, -2, 3, -1, -3)
X_ODD = (0, -1, 2, -2, 1, -3, 3)
GROUPS = ((0, 1, 2, 3, 4), (5, 6), (7,))
NT = (((1,), (1,)), ((), ()))
DUMMY = OT << 16
TLIST = LIST
POFF = TLIST + 32
TOFF = POFF + 8
FLAG = TOFF + 8
META = 384


def send(block, axis, distance):
    n = lax.axis_size(axis)
    return lax.ppermute(block, axis, [(i, (i + distance) % n) for i in range(n)])


def swap_cores(block):
    n = lax.axis_size("col")
    return lax.ppermute(block, "col", [(i, i ^ 1) for i in range(n)])


def pick(onehot, table):
    return jnp.dot(onehot.astype(jnp.int32), table, preferred_element_type=jnp.int32)


def work_list(row_index, col_index, perm, p_cols, out_pairs, flag):
    n_rows, n_cols = lax.axis_size("row"), lax.axis_size("col")
    even = (col_index % 2) == 0
    steps = jnp.where(even, jnp.array(X_EVEN, jnp.int32), jnp.array(X_ODD, jnp.int32))
    left_pos = row_index * n_cols + jnp.mod(col_index + steps, n_cols)
    right_pos = jnp.mod(row_index + jnp.array(Z_STEPS, jnp.int32), n_rows) * n_cols + col_index
    pos = jnp.concatenate([left_pos, right_pos])
    onehot = pos[:, None] == jnp.arange(perm.shape[0], dtype=jnp.int32)[None, :]
    ids = jnp.sum(jnp.where(onehot, perm[None, :], 0), axis=1)
    cols = pick(onehot, p_cols)
    nl = len(X_EVEN)
    left_hot = out_pairs[:, 0:1] == ids[None, :nl]
    right_hot = out_pairs[:, 1:2] == ids[None, nl:]
    left_cols = pick(left_hot, cols[:nl])
    right_cols = pick(right_hot, cols[nl:])
    left_at = jnp.sum(jnp.where(left_hot, jnp.arange(nl, dtype=jnp.int32)[None, :], 0), axis=1)
    right_at = jnp.sum(
        jnp.where(right_hot, jnp.arange(len(Z_STEPS), dtype=jnp.int32)[None, :], 0), axis=1
    )
    group_of = [g for row in range(len(Z_STEPS)) for g, rows in enumerate(GROUPS) if row in rows]
    group = jnp.sum(jnp.where(right_hot, jnp.array(group_of, jnp.int32)[None, :], 0), axis=1)
    slots = jnp.arange(NNZ, dtype=jnp.int32)
    match = left_cols[:, :, None] == right_cols[:, None, :]
    present = jnp.any(match, axis=2)
    partner = jnp.sum(jnp.where(match, slots[None, None, :], 0), axis=2)
    tiles = jnp.arange(OT, dtype=jnp.int32)
    payload = (
        (tiles[:, None] << 16)
        + ((left_at[:, None] * NNZ + slots[None, :]) << 8)
        + right_at[:, None] * NNZ
        + partner
    )
    count = jnp.sum(present.astype(jnp.int32), axis=1)
    earlier = (group[:, None] == group[None, :]) & (tiles[None, :] < tiles[:, None])
    row_start = jnp.sum(jnp.where(earlier, count[None, :], 0), axis=1)
    gs = jnp.arange(8, dtype=jnp.int32)
    in_group = group[None, :] == gs[:, None]
    steps_of = (jnp.sum(jnp.where(in_group, count[None, :], 0), axis=1) + UNROLL - 1) // UNROLL
    before = gs[None, :] < gs[:, None]
    step_start = jnp.sum(jnp.where(before, steps_of[None, :], 0), axis=1)
    tile_start = jnp.sum((group[None, :] < gs[:, None]).astype(jnp.int32), axis=1)
    ahead = jnp.sum(
        (present[:, None, :] & (slots[None, None, :] < slots[None, :, None])).astype(jnp.int32),
        axis=2,
    )
    group_start = jnp.sum(jnp.where(in_group, step_start[:, None], 0), axis=0) * UNROLL
    rank = jnp.where(present, group_start[:, None] + row_start[:, None] + ahead, -1)
    places = jnp.arange(LIST, dtype=jnp.int32)
    pairs = DUMMY + jnp.sum(
        jnp.where(rank[:, :, None] == places[None, None, :], payload[:, :, None] - DUMMY, 0),
        axis=(0, 1),
    )
    own_hit = left_cols == out_pairs[:, 1:2]
    own = jnp.sum(
        jnp.where(own_hit, left_at[:, None] * NNZ + slots[None, :] + 1, 0), axis=1
    )
    tile_rank = jnp.sum(
        ((group[None, :] < group[:, None]) | earlier).astype(jnp.int32), axis=1
    )
    tile_list = jnp.sum(
        jnp.where(
            tile_rank[:, None] == jnp.arange(32, dtype=jnp.int32)[None, :],
            ((tiles << 8) + own)[:, None],
            0,
        ),
        axis=0,
    )
    tail = jnp.full((META - FLAG,), flag, jnp.int32)
    return jnp.concatenate([pairs, tile_list, step_start, tile_start, tail])


def split(block):
    high = block.astype(jnp.bfloat16)
    return high, (block - high.astype(jnp.float32)).astype(jnp.bfloat16)


def product(left, right):
    lh, ll = split(left)
    rh, rl = split(right)
    a = jnp.concatenate([lh, ll], axis=1)
    b = jnp.concatenate(
        [jnp.concatenate([rh, rh], axis=1), jnp.concatenate([rl, rl], axis=1)], axis=0
    )
    both = lax.dot_general(a, b, NT, preferred_element_type=jnp.float32)
    return both[:, :BS] + both[:, BS:]


def kernel(group, n_left, sizes, first, meta, *refs):
    left = refs[:n_left]
    right = refs[n_left : n_left + len(sizes)]
    out, left_panel, right_panel, acc, in_sems, out_sems = refs[-6:]
    copies = []
    for i, ref in enumerate(left):
        copies.append((ref.at[0], left_panel.at[pl.ds(i * NNZ, NNZ)]))
    at = 0
    for ref, size in zip(right, sizes):
        copies.append((ref.at[0], right_panel.at[pl.ds(at, size)]))
        at += size
    copies = [
        pltpu.make_async_copy(src, dst, in_sems.at[i]) for i, (src, dst) in enumerate(copies)
    ]
    for copy in copies:
        copy.start()
    t0, t1 = meta[TOFF + group], meta[TOFF + group + 1]
    p0, p1 = meta[POFF + group], meta[POFF + group + 1]
    doubled = meta[FLAG] == 1

    def clear(i, _):
        acc[meta[TLIST + i] >> 8] = jnp.zeros((BS, BS), jnp.float32)
        return 0

    lax.fori_loop(t0, t1, clear, 0)
    for copy in copies:
        copy.wait()

    def pairs(step, _):
        for k in range(UNROLL):
            item = meta[step * UNROLL + k]
            tile = item >> 16
            l_at = (item >> 8) & 255
            r_at = jnp.maximum((item & 255) - first, 0)
            acc[tile] = acc[tile] + product(left_panel[l_at], right_panel[r_at])
        return 0

    lax.fori_loop(p0, p1, pairs, 0)

    def out_copy(tile):
        return pltpu.make_async_copy(acc.at[tile], out.at[tile], out_sems.at[tile])

    def finish(i, _):
        item = meta[TLIST + i]
        tile, own = item >> 8, item & 255

        @pl.when(doubled)
        def _():
            scale = jnp.where(own > 0, 2.0, 0.0)
            acc[tile] = scale * left_panel[jnp.maximum(own - 1, 0)] - acc[tile]

        out_copy(tile).start()
        return 0

    lax.fori_loop(t0, t1, finish, 0)

    def drain(i, _):
        out_copy(meta[TLIST + i] >> 8).wait()
        return 0

    lax.fori_loop(t0, t1, drain, 0)


def run_group(group, meta, left, right, previous):
    sizes = tuple(block.shape[1] for block in right)
    first = GROUPS[group][0] * NNZ
    any_spec = pl.BlockSpec(memory_space=pl.ANY)
    operands = [meta, *left, *right]
    aliases = {}
    if previous is not None:
        aliases = {len(operands): 0}
        operands.append(previous)
    work = OT * len(GROUPS[group]) // len(Z_STEPS) * 4
    return pl.pallas_call(
        functools.partial(kernel, group, len(left), sizes, first),
        out_shape=jax.ShapeDtypeStruct((OT, BS, BS), jnp.float32),
        in_specs=[pl.BlockSpec(memory_space=pltpu.SMEM)] + [any_spec] * (len(operands) - 1),
        out_specs=any_spec,
        scratch_shapes=[
            pltpu.VMEM((len(left) * NNZ, BS, BS), jnp.float32),
            pltpu.VMEM((sum(sizes), BS, BS), jnp.float32),
            pltpu.VMEM((OT + 1, BS, BS), jnp.float32),
            pltpu.SemaphoreType.DMA((len(left) + len(right),)),
            pltpu.SemaphoreType.DMA((OT,)),
        ],
        input_output_aliases=aliases,
        cost_estimate=pl.CostEstimate(
            flops=work * 8 * BS**3, bytes_accessed=10 << 20, transcendentals=0
        ),
        compiler_params=pltpu.CompilerParams(vmem_limit_bytes=24 << 20),
        name=f"pairs_{group}",
    )(*operands)


def shards(p_vals, p_cols, perm, out_pattern, branch_flag):
    row_index = lax.axis_index("row")
    col_index = lax.axis_index("col")
    halves = [p_vals[:, :HALF], p_vals[:, HALF:]]
    up, down = list(halves), list(halves)
    right = {0: [p_vals]}
    for step in range(3):
        up = [send(block, "row", 1) for block in up]
        down = [send(block, "row", -1) for block in down]
        right[2 * step + 1], right[2 * step + 2] = up, down
    right[7] = [send(up[0], "row", 1), send(down[1], "row", -1)]

    n = lax.axis_size("col")
    ahead2 = send(p_vals, "col", -2)
    behind2 = send(p_vals, "col", 2)
    relay = jnp.where((col_index % 2) == 0, ahead2, behind2)
    far = lax.ppermute(
        relay, "col", [((i - 1) % n if i % 2 == 0 else (i + 1) % n, i) for i in range(n)]
    )
    left = [
        p_vals,
        swap_cores(p_vals),
        ahead2,
        behind2,
        swap_cores(ahead2),
        swap_cores(behind2),
        far,
    ]
    meta = work_list(row_index, col_index, perm, p_cols, out_pattern[0, 0], branch_flag[0, 0])
    out = None
    for group, rows in enumerate(GROUPS):
        out = run_group(group, meta, left, [block for row in rows for block in right[row]], out)
    return out.reshape((1, 1) + out.shape)


def solution(mesh):
    return jax.shard_map(
        shards,
        mesh=mesh,
        in_specs=(
            P(("row", "col"), None, None, None),
            P(),
            P(),
            P("row", "col", None, None),
            P("row", "col"),
        ),
        out_specs=P("row", "col", None, None, None),
        check_vma=False,
    )
```

```python
import functools

import jax
import jax.numpy as jnp
from jax import lax
from jax.experimental import pallas as pl
from jax.experimental.pallas import tpu as pltpu
from jax.sharding import PartitionSpec as P

BS = 128
NNZ = 12
OT = 24
UNROLL = 4
LIST = 320
Z_EVEN = (0, -1, 1, -2, 2, -3, 3, 4)
Z_ODD = (0, 1, -1, 2, -2, 3, -3, 4)
X_EVEN = (0, 1, -2, -1, -3, 3, 2)
X_ODD = (0, -1, 2, 1, 3, -3, -2)
GROUPS = ((0, 1, 2), (3, 4), (5, 6), (7,))
NT = (((1,), (1,)), ((), ()))
DUMMY = OT << 16
TLIST = LIST
POFF = TLIST + 32
TOFF = POFF + 8
FLAG = TOFF + 8
META = 384


def swap_cores(block):
    n = lax.axis_size("col")
    return lax.ppermute(block, "col", [(i, i ^ 1) for i in range(n)])


def next_chip(block):
    n = lax.axis_size("col")
    return lax.ppermute(block, "col", [(i, (i + (-2 if i % 2 else 2)) % n) for i in range(n)])


def ring(block, turn):
    rows, cols = lax.axis_size("row"), lax.axis_size("col")
    route = []
    for r in range(rows):
        for c in range(cols):
            step = turn if c % 2 == 0 else -turn
            route.append((r * cols + c, (r + step) % rows * cols + c))
    return lax.ppermute(block, ("row", "col"), route)


def after(block, *others):
    return lax.optimization_barrier((block, others))[0]


def hold(block, token):
    return lax.optimization_barrier((block, token))


def pick(onehot, table):
    return jnp.dot(onehot.astype(jnp.int32), table, preferred_element_type=jnp.int32)


def work_list(row_index, col_index, perm, p_cols, out_pairs, flag):
    n_rows, n_cols = lax.axis_size("row"), lax.axis_size("col")
    even = (col_index % 2) == 0
    steps = jnp.where(even, jnp.array(X_EVEN, jnp.int32), jnp.array(X_ODD, jnp.int32))
    left_pos = row_index * n_cols + jnp.mod(col_index + steps, n_cols)
    turns = jnp.where(even, jnp.array(Z_EVEN, jnp.int32), jnp.array(Z_ODD, jnp.int32))
    right_pos = jnp.mod(row_index + turns, n_rows) * n_cols + col_index
    pos = jnp.concatenate([left_pos, right_pos])
    onehot = pos[:, None] == jnp.arange(perm.shape[0], dtype=jnp.int32)[None, :]
    ids = jnp.sum(jnp.where(onehot, perm[None, :], 0), axis=1)
    cols = pick(onehot, p_cols)
    nl = len(X_EVEN)
    left_hot = out_pairs[:, 0:1] == ids[None, :nl]
    right_hot = out_pairs[:, 1:2] == ids[None, nl:]
    left_cols = pick(left_hot, cols[:nl])
    right_cols = pick(right_hot, cols[nl:])
    left_at = jnp.sum(jnp.where(left_hot, jnp.arange(nl, dtype=jnp.int32)[None, :], 0), axis=1)
    right_at = jnp.sum(
        jnp.where(right_hot, jnp.arange(len(Z_EVEN), dtype=jnp.int32)[None, :], 0), axis=1
    )
    group_of = [g for row in range(len(Z_EVEN)) for g, rows in enumerate(GROUPS) if row in rows]
    group = jnp.sum(jnp.where(right_hot, jnp.array(group_of, jnp.int32)[None, :], 0), axis=1)
    slots = jnp.arange(NNZ, dtype=jnp.int32)
    match = left_cols[:, :, None] == right_cols[:, None, :]
    present = jnp.any(match, axis=2)
    partner = jnp.sum(jnp.where(match, slots[None, None, :], 0), axis=2)
    tiles = jnp.arange(OT, dtype=jnp.int32)
    payload = (
        (tiles[:, None] << 16)
        + ((left_at[:, None] * NNZ + slots[None, :]) << 8)
        + right_at[:, None] * NNZ
        + partner
    )
    count = jnp.sum(present.astype(jnp.int32), axis=1)
    earlier = (group[:, None] == group[None, :]) & (tiles[None, :] < tiles[:, None])
    row_start = jnp.sum(jnp.where(earlier, count[None, :], 0), axis=1)
    gs = jnp.arange(8, dtype=jnp.int32)
    in_group = group[None, :] == gs[:, None]
    steps_of = (jnp.sum(jnp.where(in_group, count[None, :], 0), axis=1) + UNROLL - 1) // UNROLL
    before = gs[None, :] < gs[:, None]
    step_start = jnp.sum(jnp.where(before, steps_of[None, :], 0), axis=1)
    tile_start = jnp.sum((group[None, :] < gs[:, None]).astype(jnp.int32), axis=1)
    ahead = jnp.sum(
        (present[:, None, :] & (slots[None, None, :] < slots[None, :, None])).astype(jnp.int32),
        axis=2,
    )
    group_start = jnp.sum(jnp.where(in_group, step_start[:, None], 0), axis=0) * UNROLL
    rank = jnp.where(present, group_start[:, None] + row_start[:, None] + ahead, -1)
    places = jnp.arange(LIST, dtype=jnp.int32)
    pairs = DUMMY + jnp.sum(
        jnp.where(rank[:, :, None] == places[None, None, :], payload[:, :, None] - DUMMY, 0),
        axis=(0, 1),
    )
    own_hit = left_cols == out_pairs[:, 1:2]
    own = jnp.sum(
        jnp.where(own_hit, left_at[:, None] * NNZ + slots[None, :] + 1, 0), axis=1
    )
    tile_rank = jnp.sum(
        ((group[None, :] < group[:, None]) | earlier).astype(jnp.int32), axis=1
    )
    tile_list = jnp.sum(
        jnp.where(
            tile_rank[:, None] == jnp.arange(32, dtype=jnp.int32)[None, :],
            ((tiles << 8) + own)[:, None],
            0,
        ),
        axis=0,
    )
    tail = jnp.full((META - FLAG,), flag, jnp.int32)
    return jnp.concatenate([pairs, tile_list, step_start, tile_start, tail]), ids


def split(block):
    high = block.astype(jnp.bfloat16)
    return high, (block - high.astype(jnp.float32)).astype(jnp.bfloat16)


def fetch(refs, rows, sems):
    copies = [pltpu.make_async_copy(ref.at[0], rows.at[i], sems.at[i]) for i, ref in enumerate(refs)]
    for copy in copies:
        copy.start()
    return copies


def prepare(n_left, meta, *refs):
    panel, base, token, rows, sems = refs[n_left:]
    token[...] = jnp.zeros_like(token)
    copies = fetch(refs[:n_left], rows, sems)
    for row, copy in enumerate(copies):
        copy.wait()

        def block(s, _, row=row):
            high, low = split(rows[row, s])
            panel[row * NNZ + s, :, :BS] = high
            panel[row * NNZ + s, :, BS:] = low
            return 0

        lax.fori_loop(0, NNZ, block, 0)
    doubled = meta[FLAG] == 1

    def own(i, _):
        item = meta[TLIST + i]
        tile, at = item >> 8, (item & 255) - 1
        scale = jnp.where((at >= 0) & doubled, 2.0, 0.0)
        at = jnp.maximum(at, 0)
        base[tile] = scale * rows[at // NNZ, at % NNZ]
        return 0

    lax.fori_loop(0, OT, own, 0)
    base[OT] = jnp.zeros((BS, BS), jnp.float32)


def split_rows(right, rows, right_panel, sems):
    copies = fetch(right, rows, sems)
    for row, copy in enumerate(copies):
        copy.wait()

        def block(s, _, row=row):
            high, low = split(rows[row, s])
            right_panel[row * NNZ + s, :BS] = high
            right_panel[row * NNZ + s, BS:] = low
            return 0

        lax.fori_loop(0, NNZ, block, 0)


def add_pairs(group, meta, panel, right_panel, acc):
    first = GROUPS[group][0] * NNZ
    sign = jnp.where(meta[FLAG] == 1, -1.0, 1.0)

    def pairs(step, _):
        for k in range(UNROLL):
            item = meta[step * UNROLL + k]
            tile = item >> 16
            l_at = (item >> 8) & 255
            r_at = jnp.maximum((item & 255) - first, 0)
            r = right_panel[r_at]
            both = lax.dot_general(
                panel[l_at],
                jnp.concatenate([r, r], axis=1),
                NT,
                preferred_element_type=jnp.float32,
            )
            acc[tile] = acc[tile] + sign * (both[:, :BS] + both[:, BS:])
        return 0

    lax.fori_loop(meta[POFF + group], meta[POFF + group + 1], pairs, 0)


def kernel(group, n_right, meta, panel, base, *refs):
    total, token, rows, right_panel, sems = refs[-5:]
    token[...] = jnp.zeros_like(token)
    split_rows(refs[:n_right], rows, right_panel, sems)
    add_pairs(group, meta, panel, right_panel, total)


def last_kernel(group, n_right, meta, panel, base, *refs):
    out, rows, right_panel, acc, sems, out_sems, all_sem = refs[-7:]
    whole = pltpu.make_async_copy(base.at[pl.ds(0, OT)], out, all_sem)
    whole.start()
    t0, t1 = meta[TOFF + group], meta[TOFF + group + 1]

    def begin(i, _):
        tile = meta[TLIST + i] >> 8
        acc[tile] = base[tile]
        return 0

    lax.fori_loop(t0, t1, begin, 0)
    acc[OT] = jnp.zeros((BS, BS), jnp.float32)
    split_rows(refs[:n_right], rows, right_panel, sems)
    add_pairs(group, meta, panel, right_panel, acc)
    whole.wait()

    def out_copy(i):
        tile = meta[TLIST + i] >> 8
        return pltpu.make_async_copy(acc.at[tile], out.at[tile], out_sems.at[tile])

    def leave(i, _):
        out_copy(i).start()
        return 0

    def drain(i, _):
        out_copy(i).wait()
        return 0

    lax.fori_loop(t0, t1, leave, 0)
    lax.fori_loop(t0, t1, drain, 0)


def in_hbm(blocks):
    return [pltpu.with_memory_space_constraint(block, pltpu.HBM) for block in blocks]


VMEM_SPEC = pl.BlockSpec(memory_space=pltpu.VMEM)
SMEM_SPEC = pl.BlockSpec(memory_space=pltpu.SMEM)
TOTAL = pltpu.VMEM((OT + 1, BS, BS), jnp.float32)
TOKEN = jax.ShapeDtypeStruct((8, BS), jnp.float32)
ANY_SPEC = pl.BlockSpec(memory_space=pl.ANY)


def run_prepare(meta, left):
    return pl.pallas_call(
        functools.partial(prepare, len(left)),
        out_shape=[
            pltpu.VMEM((len(left) * NNZ, BS, 2 * BS), jnp.bfloat16),
            TOTAL,
            TOKEN,
        ],
        in_specs=[SMEM_SPEC] + [ANY_SPEC] * len(left),
        out_specs=[VMEM_SPEC, VMEM_SPEC, VMEM_SPEC],
        scratch_shapes=[
            pltpu.VMEM((len(left), NNZ, BS, BS), jnp.float32),
            pltpu.SemaphoreType.DMA((len(left),)),
        ],
        cost_estimate=pl.CostEstimate(
            flops=5 << 20, bytes_accessed=12 << 20, transcendentals=0
        ),
        compiler_params=pltpu.CompilerParams(vmem_limit_bytes=16 << 20),
        name="left_panel",
    )(meta, *in_hbm(left))


def run_group(group, meta, panel, base, right, order):
    last = group == len(GROUPS) - 1
    if group < 2:
        right = in_hbm(right)
    operands = [meta, panel, base, *right, order]
    row_sems = pltpu.SemaphoreType.DMA((len(right),))
    scratch = [
        pltpu.VMEM((len(right), NNZ, BS, BS), jnp.float32),
        pltpu.VMEM((len(right) * NNZ, 2 * BS, BS), jnp.bfloat16),
    ]
    if last:
        scratch += [pltpu.VMEM((OT + 1, BS, BS), jnp.float32), row_sems]
        scratch += [pltpu.SemaphoreType.DMA((OT,)), pltpu.SemaphoreType.DMA]
    else:
        scratch += [row_sems]
    work = OT * len(right) // len(Z_EVEN) * 4
    return pl.pallas_call(
        functools.partial(last_kernel if last else kernel, group, len(right)),
        out_shape=jax.ShapeDtypeStruct((OT, BS, BS), jnp.float32) if last else [TOTAL, TOKEN],
        in_specs=[SMEM_SPEC, VMEM_SPEC, VMEM_SPEC] + [ANY_SPEC] * (len(right) + 1),
        out_specs=ANY_SPEC if last else [VMEM_SPEC, VMEM_SPEC],
        scratch_shapes=scratch,
        input_output_aliases={} if last else {2: 0},
        cost_estimate=pl.CostEstimate(
            flops=work * 8 * BS**3, bytes_accessed=4 << 20, transcendentals=0
        ),
        compiler_params=pltpu.CompilerParams(vmem_limit_bytes=16 << 20),
        name=f"pairs_{group}",
    )(*operands)


def shards(p_vals, p_cols, perm, out_pattern, branch_flag):
    row_index = lax.axis_index("row")
    col_index = lax.axis_index("col")
    meta, ids = work_list(row_index, col_index, perm, p_cols, out_pattern[0, 0], branch_flag[0, 0])

    one1 = ring(p_vals, 1)
    partner = swap_cores(p_vals)
    near = next_chip(p_vals)
    other1 = ring(after(p_vals, ids), -1)
    near_partner = next_chip(partner)
    one2 = ring(one1, 1)
    near_swapped = swap_cores(after(near, one1))
    other2 = ring(after(other1, near_partner), -1)
    far_partner = next_chip(near_partner)
    near_partner_swapped = swap_cores(near_partner)
    one3 = ring(one2, 1)
    panel, base, token = run_prepare(
        meta,
        [p_vals, partner, near, near_partner, far_partner, near_swapped, near_partner_swapped],
    )
    other3 = ring(other2, -1)
    before4, token = hold(one3, token)
    one4 = ring(before4, 1)
    total, token = run_group(0, meta, panel, base, [p_vals, one1, other1], token)
    total, token = run_group(1, meta, panel, total, [one2, other2], token)
    total, token = run_group(2, meta, panel, total, [one3, other3], token)
    out = run_group(3, meta, panel, total, [one4], token)
    return out.reshape((1, 1) + out.shape)


def solution(mesh):
    return jax.shard_map(
        shards,
        mesh=mesh,
        in_specs=(
            P(("row", "col"), None, None, None),
            P(),
            P(),
            P("row", "col", None, None),
            P("row", "col"),
        ),
        out_specs=P("row", "col", None, None, None),
        check_vma=False,
    )
```

```python
import functools

import jax
import jax.numpy as jnp
from jax import lax
from jax.experimental import pallas as pl
from jax.experimental.pallas import tpu as pltpu
from jax.sharding import PartitionSpec as P

BS = 128
NNZ = 12
OT = 24
HALF = NNZ // 2
UNROLL = 4
LIST = 320
Z_EVEN = (-1, 1, 0, -2, 2, -3, 3, 4)
Z_ODD = (1, -1, 0, 2, -2, 3, -3, 4)
X_EVEN = (0, 1, -2, -1, -3, 3, 2)
X_ODD = (0, -1, 2, 1, 3, -3, -2)
GROUPS = ((0, 1, 2), (3, 4), (5, 6), (7,))
NT = (((1,), (1,)), ((), ()))
DUMMY = OT << 16
TLIST = LIST
POFF = TLIST + 32
TOFF = POFF + 8
FLAG = TOFF + 8
META = 384


def swap_cores(block):
    n = lax.axis_size("col")
    return lax.ppermute(block, "col", [(i, i ^ 1) for i in range(n)])


def next_chip(block):
    n = lax.axis_size("col")
    return lax.ppermute(block, "col", [(i, (i + (-2 if i % 2 else 2)) % n) for i in range(n)])


def ring(block, turn):
    rows, cols = lax.axis_size("row"), lax.axis_size("col")
    route = []
    for r in range(rows):
        for c in range(cols):
            step = turn if c % 2 == 0 else -turn
            route.append((r * cols + c, (r + step) % rows * cols + c))
    return lax.ppermute(block, ("row", "col"), route)


def after(block, *others):
    return lax.optimization_barrier((block, others))[0]


def hold(block, token):
    return lax.optimization_barrier((block, token))


def pick(onehot, table):
    return jnp.dot(onehot.astype(jnp.int32), table, preferred_element_type=jnp.int32)


def work_list(row_index, col_index, perm, p_cols, out_pairs, flag):
    n_rows, n_cols = lax.axis_size("row"), lax.axis_size("col")
    even = (col_index % 2) == 0
    steps = jnp.where(even, jnp.array(X_EVEN, jnp.int32), jnp.array(X_ODD, jnp.int32))
    left_pos = row_index * n_cols + jnp.mod(col_index + steps, n_cols)
    turns = jnp.where(even, jnp.array(Z_EVEN, jnp.int32), jnp.array(Z_ODD, jnp.int32))
    right_pos = jnp.mod(row_index + turns, n_rows) * n_cols + col_index
    pos = jnp.concatenate([left_pos, right_pos])
    onehot = pos[:, None] == jnp.arange(perm.shape[0], dtype=jnp.int32)[None, :]
    ids = jnp.sum(jnp.where(onehot, perm[None, :], 0), axis=1)
    cols = pick(onehot, p_cols)
    nl = len(X_EVEN)
    left_hot = out_pairs[:, 0:1] == ids[None, :nl]
    right_hot = out_pairs[:, 1:2] == ids[None, nl:]
    left_cols = pick(left_hot, cols[:nl])
    right_cols = pick(right_hot, cols[nl:])
    left_at = jnp.sum(jnp.where(left_hot, jnp.arange(nl, dtype=jnp.int32)[None, :], 0), axis=1)
    right_at = jnp.sum(
        jnp.where(right_hot, jnp.arange(len(Z_EVEN), dtype=jnp.int32)[None, :], 0), axis=1
    )
    group_of = [g for row in range(len(Z_EVEN)) for g, rows in enumerate(GROUPS) if row in rows]
    group = jnp.sum(jnp.where(right_hot, jnp.array(group_of, jnp.int32)[None, :], 0), axis=1)
    slots = jnp.arange(NNZ, dtype=jnp.int32)
    match = left_cols[:, :, None] == right_cols[:, None, :]
    present = jnp.any(match, axis=2)
    partner = jnp.sum(jnp.where(match, slots[None, None, :], 0), axis=2)
    tiles = jnp.arange(OT, dtype=jnp.int32)
    payload = (
        (tiles[:, None] << 16)
        + ((left_at[:, None] * NNZ + slots[None, :]) << 8)
        + right_at[:, None] * NNZ
        + partner
    )
    count = jnp.sum(present.astype(jnp.int32), axis=1)
    earlier = (group[:, None] == group[None, :]) & (tiles[None, :] < tiles[:, None])
    row_start = jnp.sum(jnp.where(earlier, count[None, :], 0), axis=1)
    gs = jnp.arange(8, dtype=jnp.int32)
    in_group = group[None, :] == gs[:, None]
    steps_of = (jnp.sum(jnp.where(in_group, count[None, :], 0), axis=1) + UNROLL - 1) // UNROLL
    before = gs[None, :] < gs[:, None]
    step_start = jnp.sum(jnp.where(before, steps_of[None, :], 0), axis=1)
    tile_start = jnp.sum((group[None, :] < gs[:, None]).astype(jnp.int32), axis=1)
    ahead = jnp.sum(
        (present[:, None, :] & (slots[None, None, :] < slots[None, :, None])).astype(jnp.int32),
        axis=2,
    )
    group_start = jnp.sum(jnp.where(in_group, step_start[:, None], 0), axis=0) * UNROLL
    rank = jnp.where(present, group_start[:, None] + row_start[:, None] + ahead, -1)
    places = jnp.arange(LIST, dtype=jnp.int32)
    pairs = DUMMY + jnp.sum(
        jnp.where(rank[:, :, None] == places[None, None, :], payload[:, :, None] - DUMMY, 0),
        axis=(0, 1),
    )
    own_hit = left_cols == out_pairs[:, 1:2]
    own = jnp.sum(
        jnp.where(own_hit, left_at[:, None] * NNZ + slots[None, :] + 1, 0), axis=1
    )
    tile_rank = jnp.sum(
        ((group[None, :] < group[:, None]) | earlier).astype(jnp.int32), axis=1
    )
    tile_list = jnp.sum(
        jnp.where(
            tile_rank[:, None] == jnp.arange(32, dtype=jnp.int32)[None, :],
            ((tiles << 8) + own)[:, None],
            0,
        ),
        axis=0,
    )
    tail = jnp.full((META - FLAG,), flag, jnp.int32)
    return jnp.concatenate([pairs, tile_list, step_start, tile_start, tail]), ids


def split(block):
    high = block.astype(jnp.bfloat16)
    return high, (block - high.astype(jnp.float32)).astype(jnp.bfloat16)


def prepare(n_left, meta, *refs):
    left = refs[:n_left]
    panel, base, token, rows, sems = refs[-5:]
    token[...] = jnp.zeros_like(token)
    copies = [
        pltpu.make_async_copy(ref.at[0], rows.at[pl.ds(i * NNZ, NNZ)], sems.at[i])
        for i, ref in enumerate(left)
    ]
    for copy in copies:
        copy.start()

    def clear(tile, _):
        base[tile] = jnp.zeros((BS, BS), jnp.float32)
        return 0

    lax.fori_loop(0, OT + 1, clear, 0)
    for row, copy in enumerate(copies):
        copy.wait()

        def block(at, _):
            high, low = split(rows[at])
            panel[at, :, :BS] = high
            panel[at, :, BS:] = low
            return 0

        lax.fori_loop(row * NNZ, (row + 1) * NNZ, block, 0)
    doubled = meta[FLAG] == 1

    def own(i, _):
        item = meta[TLIST + i]
        tile, at = item >> 8, (item & 255) - 1

        @pl.when((at >= 0) & doubled)
        def _():
            base[tile] = 2.0 * rows[at]

        return 0

    lax.fori_loop(0, OT, own, 0)


def split_rows(right, right_panel, own=None):
    first = 0
    if own is not None:
        source, rows, sem = own
        copy = pltpu.make_async_copy(source.at[0], rows, sem)
        copy.start()
    for ref in right:
        split_row(ref.at[0], first, ref.shape[1], right_panel)
        first += ref.shape[1]
    if own is not None:
        copy.wait()
        split_row(rows, first, NNZ, right_panel)


def split_row(blocks, first, size, right_panel):
    def block(at, _):
        high, low = split(blocks[at])
        right_panel[first + at, :BS] = high
        right_panel[first + at, BS:] = low
        return 0

    lax.fori_loop(0, size, block, 0)


def add_pairs(group, meta, panel, right_panel, acc):
    first = GROUPS[group][0] * NNZ
    sign = jnp.where(meta[FLAG] == 1, -1.0, 1.0)

    def pairs(step, _):
        for k in range(UNROLL):
            item = meta[step * UNROLL + k]
            tile = item >> 16
            l_at = (item >> 8) & 255
            r_at = jnp.maximum((item & 255) - first, 0)
            r = right_panel[r_at]
            both = lax.dot_general(
                panel[l_at],
                jnp.concatenate([r, r], axis=1),
                NT,
                preferred_element_type=jnp.float32,
            )
            acc[tile] = acc[tile] + sign * (both[:, :BS] + both[:, BS:])
        return 0

    lax.fori_loop(meta[POFF + group], meta[POFF + group + 1], pairs, 0)


def kernel(group, n_right, meta, panel, base, *refs):
    own = None
    if group == 0:
        own, refs = (refs[n_right], *refs[-2:]), refs[:-2]
    total, token, right_panel = refs[-3:]
    token[...] = jnp.zeros_like(token)
    split_rows(refs[:n_right], right_panel, own)
    add_pairs(group, meta, panel, right_panel, total)


def last_kernel(group, n_right, meta, panel, base, *refs):
    out, right_panel, acc, out_sems, all_sem = refs[-5:]
    whole = pltpu.make_async_copy(base.at[pl.ds(0, OT)], out, all_sem)
    whole.start()
    t0, t1 = meta[TOFF + group], meta[TOFF + group + 1]

    def begin(i, _):
        tile = meta[TLIST + i] >> 8
        acc[tile] = base[tile]
        return 0

    lax.fori_loop(t0, t1, begin, 0)
    acc[OT] = jnp.zeros((BS, BS), jnp.float32)
    split_rows(refs[:n_right], right_panel)
    add_pairs(group, meta, panel, right_panel, acc)
    whole.wait()

    def out_copy(i):
        tile = meta[TLIST + i] >> 8
        return pltpu.make_async_copy(acc.at[tile], out.at[tile], out_sems.at[tile])

    def leave(i, _):
        out_copy(i).start()
        return 0

    def drain(i, _):
        out_copy(i).wait()
        return 0

    lax.fori_loop(t0, t1, leave, 0)
    lax.fori_loop(t0, t1, drain, 0)


VMEM_SPEC = pl.BlockSpec(memory_space=pltpu.VMEM)
SMEM_SPEC = pl.BlockSpec(memory_space=pltpu.SMEM)
TOTAL = pltpu.VMEM((OT + 1, BS, BS), jnp.float32)
TOKEN = jax.ShapeDtypeStruct((8, BS), jnp.float32)
ANY_SPEC = pl.BlockSpec(memory_space=pl.ANY)


def in_hbm(block):
    return pltpu.with_memory_space_constraint(block, pltpu.HBM)


def run_prepare(meta, left):
    return pl.pallas_call(
        functools.partial(prepare, len(left)),
        out_shape=[
            pltpu.VMEM((len(left) * NNZ, BS, 2 * BS), jnp.bfloat16),
            TOTAL,
            TOKEN,
        ],
        in_specs=[SMEM_SPEC] + [ANY_SPEC] * len(left),
        out_specs=[VMEM_SPEC, VMEM_SPEC, VMEM_SPEC],
        scratch_shapes=[
            pltpu.VMEM((len(left) * NNZ, BS, BS), jnp.float32),
            pltpu.SemaphoreType.DMA((len(left),)),
        ],
        cost_estimate=pl.CostEstimate(
            flops=5 << 20, bytes_accessed=12 << 20, transcendentals=0
        ),
        compiler_params=pltpu.CompilerParams(vmem_limit_bytes=16 << 20),
        name="left_panel",
    )(meta, *[in_hbm(block) for block in left])


def run_group(group, meta, panel, base, right, order, own=None):
    last = group == len(GROUPS) - 1
    blocks = sum(block.shape[1] for block in right)
    extra = [order] if own is None else [in_hbm(own), order]
    scratch = [pltpu.VMEM((len(GROUPS[group]) * NNZ, 2 * BS, BS), jnp.bfloat16)]
    if last:
        scratch += [pltpu.VMEM((OT + 1, BS, BS), jnp.float32)]
        scratch += [pltpu.SemaphoreType.DMA((OT,)), pltpu.SemaphoreType.DMA]
    if own is not None:
        scratch += [pltpu.VMEM((NNZ, BS, BS), jnp.float32), pltpu.SemaphoreType.DMA]
    return pl.pallas_call(
        functools.partial(last_kernel if last else kernel, group, len(right)),
        out_shape=jax.ShapeDtypeStruct((OT, BS, BS), jnp.float32) if last else [TOTAL, TOKEN],
        in_specs=[SMEM_SPEC] + [VMEM_SPEC] * (len(right) + 2) + [ANY_SPEC] * len(extra),
        out_specs=ANY_SPEC if last else [VMEM_SPEC, VMEM_SPEC],
        scratch_shapes=scratch,
        input_output_aliases={} if last else {2: 0},
        cost_estimate=pl.CostEstimate(
            flops=blocks * 16 * BS**3, bytes_accessed=4 << 20, transcendentals=0
        ),
        compiler_params=pltpu.CompilerParams(vmem_limit_bytes=16 << 20),
        name=f"pairs_{group}",
    )(meta, panel, base, *right, *extra)


def shards(p_vals, p_cols, perm, out_pattern, branch_flag):
    row_index = lax.axis_index("row")
    col_index = lax.axis_index("col")
    meta, ids = work_list(row_index, col_index, perm, p_cols, out_pattern[0, 0], branch_flag[0, 0])

    one1 = ring(p_vals, 1)
    partner = swap_cores(p_vals)
    other1 = ring(after(p_vals, ids), -1)
    near = next_chip(after(p_vals, partner))
    near_partner = next_chip(partner)
    one2 = ring(one1, 1)
    near_swapped = swap_cores(after(near, one1))
    other2 = ring(after(other1, near_partner, meta), -1)
    far_partner = next_chip(near_partner)
    near_partner_swapped = swap_cores(near_partner)
    one2_low, one2_high = one2[:, :HALF], one2[:, HALF:]
    other2_low, other2_high = other2[:, :HALF], other2[:, HALF:]
    one3_low = ring(one2_low, 1)
    other3_high = ring(other2_high, -1)
    one3_high = ring(after(one2_high, other2), 1)
    other3_low = ring(other2_low, -1)
    panel, base, token = run_prepare(
        meta,
        [p_vals, partner, near, near_partner, far_partner, near_swapped, near_partner_swapped],
    )
    before4, token = hold(one3_low, token)
    one4_low = ring(before4, 1)
    other4_high = ring(other3_high, -1)
    total, token = run_group(0, meta, panel, base, [one1, other1], token, p_vals)
    total, token = run_group(1, meta, panel, total, [one2, other2], token)
    total, token = run_group(
        2, meta, panel, total, [one3_low, one3_high, other3_low, other3_high], token
    )
    out = run_group(3, meta, panel, total, [one4_low, other4_high], token)
    return out.reshape((1, 1) + out.shape)


def solution(mesh):
    return jax.shard_map(
        shards,
        mesh=mesh,
        in_specs=(
            P(("row", "col"), None, None, None),
            P(),
            P(),
            P("row", "col", None, None),
            P("row", "col"),
        ),
        out_specs=P("row", "col", None, None, None),
        check_vma=False,
    )
```

```python
import functools

import jax
import jax.numpy as jnp
from jax import lax
from jax.experimental import pallas as pl
from jax.experimental.pallas import tpu as pltpu
from jax.sharding import PartitionSpec as P

BS = 128
NNZ = 12
OT = 24
HALF = NNZ // 2
UNROLL = 4
LIST = 320
Z_EVEN = (-1, 1, 0, -2, 2, -3, 3, 4)
Z_ODD = (1, -1, 0, 2, -2, 3, -3, 4)
X_EVEN = (0, 1, -2, -1, -3, 3, 2)
X_ODD = (0, -1, 2, 1, 3, -3, -2)
GROUPS = ((0, 1, 2), (3, 4), (5, 6), (7,))
NT = (((1,), (1,)), ((), ()))
DUMMY = OT << 16
TLIST = LIST
POFF = TLIST + 32
TOFF = POFF + 8
FLAG = TOFF + 8
META = 384


def swap_cores(block):
    n = lax.axis_size("col")
    return lax.ppermute(block, "col", [(i, i ^ 1) for i in range(n)])


def next_chip(block):
    n = lax.axis_size("col")
    return lax.ppermute(block, "col", [(i, (i + (-2 if i % 2 else 2)) % n) for i in range(n)])


def ring(block, turn):
    rows, cols = lax.axis_size("row"), lax.axis_size("col")
    route = []
    for r in range(rows):
        for c in range(cols):
            step = turn if c % 2 == 0 else -turn
            route.append((r * cols + c, (r + step) % rows * cols + c))
    return lax.ppermute(block, ("row", "col"), route)


def after(block, *others):
    return lax.optimization_barrier((block, others))[0]


def hold(block, token):
    return lax.optimization_barrier((block, token))


def pick(onehot, table):
    return jnp.dot(onehot.astype(jnp.int32), table, preferred_element_type=jnp.int32)


def work_list(row_index, col_index, perm, p_cols, out_pairs, flag):
    n_rows, n_cols = lax.axis_size("row"), lax.axis_size("col")
    even = (col_index % 2) == 0
    steps = jnp.where(even, jnp.array(X_EVEN, jnp.int32), jnp.array(X_ODD, jnp.int32))
    left_pos = row_index * n_cols + jnp.mod(col_index + steps, n_cols)
    turns = jnp.where(even, jnp.array(Z_EVEN, jnp.int32), jnp.array(Z_ODD, jnp.int32))
    right_pos = jnp.mod(row_index + turns, n_rows) * n_cols + col_index
    pos = jnp.concatenate([left_pos, right_pos])
    onehot = pos[:, None] == jnp.arange(perm.shape[0], dtype=jnp.int32)[None, :]
    ids = jnp.sum(jnp.where(onehot, perm[None, :], 0), axis=1)
    cols = pick(onehot, p_cols)
    nl = len(X_EVEN)
    left_hot = out_pairs[:, 0:1] == ids[None, :nl]
    right_hot = out_pairs[:, 1:2] == ids[None, nl:]
    left_cols = pick(left_hot, cols[:nl])
    right_cols = pick(right_hot, cols[nl:])
    left_at = jnp.sum(jnp.where(left_hot, jnp.arange(nl, dtype=jnp.int32)[None, :], 0), axis=1)
    right_at = jnp.sum(
        jnp.where(right_hot, jnp.arange(len(Z_EVEN), dtype=jnp.int32)[None, :], 0), axis=1
    )
    group_of = [g for row in range(len(Z_EVEN)) for g, rows in enumerate(GROUPS) if row in rows]
    group = jnp.sum(jnp.where(right_hot, jnp.array(group_of, jnp.int32)[None, :], 0), axis=1)
    slots = jnp.arange(NNZ, dtype=jnp.int32)
    match = left_cols[:, :, None] == right_cols[:, None, :]
    present = jnp.any(match, axis=2)
    partner = jnp.sum(jnp.where(match, slots[None, None, :], 0), axis=2)
    tiles = jnp.arange(OT, dtype=jnp.int32)
    payload = (
        (tiles[:, None] << 16)
        + ((left_at[:, None] * NNZ + slots[None, :]) << 8)
        + right_at[:, None] * NNZ
        + partner
    )
    count = jnp.sum(present.astype(jnp.int32), axis=1)
    earlier = (group[:, None] == group[None, :]) & (tiles[None, :] < tiles[:, None])
    row_start = jnp.sum(jnp.where(earlier, count[None, :], 0), axis=1)
    gs = jnp.arange(8, dtype=jnp.int32)
    in_group = group[None, :] == gs[:, None]
    steps_of = (jnp.sum(jnp.where(in_group, count[None, :], 0), axis=1) + UNROLL - 1) // UNROLL
    before = gs[None, :] < gs[:, None]
    step_start = jnp.sum(jnp.where(before, steps_of[None, :], 0), axis=1)
    tile_start = jnp.sum((group[None, :] < gs[:, None]).astype(jnp.int32), axis=1)
    ahead = jnp.sum(
        (present[:, None, :] & (slots[None, None, :] < slots[None, :, None])).astype(jnp.int32),
        axis=2,
    )
    group_start = jnp.sum(jnp.where(in_group, step_start[:, None], 0), axis=0) * UNROLL
    rank = jnp.where(present, group_start[:, None] + row_start[:, None] + ahead, -1)
    places = jnp.arange(LIST, dtype=jnp.int32)
    pairs = DUMMY + jnp.sum(
        jnp.where(rank[:, :, None] == places[None, None, :], payload[:, :, None] - DUMMY, 0),
        axis=(0, 1),
    )
    own_hit = left_cols == out_pairs[:, 1:2]
    own = jnp.sum(
        jnp.where(own_hit, left_at[:, None] * NNZ + slots[None, :] + 1, 0), axis=1
    )
    tile_rank = jnp.sum(
        ((group[None, :] < group[:, None]) | earlier).astype(jnp.int32), axis=1
    )
    tile_list = jnp.sum(
        jnp.where(
            tile_rank[:, None] == jnp.arange(32, dtype=jnp.int32)[None, :],
            ((tiles << 8) + own)[:, None],
            0,
        ),
        axis=0,
    )
    tail = jnp.full((META - FLAG,), flag, jnp.int32)
    return jnp.concatenate([pairs, tile_list, step_start, tile_start, tail]), ids


def split(block):
    high = block.astype(jnp.bfloat16)
    return high, (block - high.astype(jnp.float32)).astype(jnp.bfloat16)


def prepare(n_left, meta, *refs):
    left = refs[:n_left]
    panel, base, token = refs[n_left:]
    token[...] = jnp.zeros_like(token)
    use = meta[FLAG] == 1

    def clear(tile, _):
        base[tile] = jnp.zeros((BS, BS), jnp.float32)
        return 0

    lax.fori_loop(0, OT + 1, clear, 0)
    for row, ref in enumerate(left):

        def block(at, _, row=row, ref=ref):
            high, low = split(ref[0, at])
            panel[row * NNZ + at, :, :BS] = high
            panel[row * NNZ + at, :, BS:] = low
            return 0

        lax.fori_loop(0, NNZ, block, 0)

    @pl.when(use)
    def _():
        def own(i, _):
            item = meta[TLIST + i]
            tile, at = item >> 8, (item & 255) - 1
            for row, ref in enumerate(left):

                @pl.when((at >= row * NNZ) & (at < (row + 1) * NNZ))
                def _(row=row, ref=ref):
                    base[tile] = 2.0 * ref[0, at - row * NNZ]

            return 0

        lax.fori_loop(0, OT, own, 0)


def split_rows(right, right_panel):
    first = 0
    for ref in right:
        split_row(ref.at[0], first, ref.shape[1], right_panel)
        first += ref.shape[1]
    return first


def split_row(blocks, first, size, right_panel):
    def block(at, _):
        high, low = split(blocks[at])
        right_panel[first + at, :BS] = high
        right_panel[first + at, BS:] = low
        return 0

    lax.fori_loop(0, size, block, 0)


def add_pairs(group, meta, panel, right_panel, acc):
    first = GROUPS[group][0] * NNZ
    sign = jnp.where(meta[FLAG] == 1, -1.0, 1.0)

    def some(at, count):
        for k in range(count):
            item = meta[at + k]
            tile = item >> 16
            l_at = (item >> 8) & 255
            r_at = jnp.maximum((item & 255) - first, 0)
            r = right_panel[r_at]
            both = lax.dot_general(
                panel[l_at],
                jnp.concatenate([r, r], axis=1),
                NT,
                preferred_element_type=jnp.float32,
            )
            acc[tile] = acc[tile] + sign * (both[:, :BS] + both[:, BS:])

    start, end = meta[POFF + group], meta[POFF + group + 1]

    def pairs(step, _):
        some((start + 2 * step) * UNROLL, 2 * UNROLL)
        return 0

    lax.fori_loop(0, (end - start) // 2, pairs, 0)

    @pl.when((end - start) % 2 == 1)
    def _():
        some((end - 1) * UNROLL, UNROLL)


def tile_copy(meta, source, out, sems, i):
    tile = meta[TLIST + i] >> 8
    return pltpu.make_async_copy(source.at[tile], out.at[tile], sems.at[tile])


def send_tiles(meta, source, out, sems, first, last):
    def leave(i, _):
        tile_copy(meta, source, out, sems, i).start()
        return 0

    lax.fori_loop(first, last, leave, 0)


def wait_tiles(meta, source, out, sems, first, last):
    def drain(i, _):
        tile_copy(meta, source, out, sems, i).wait()
        return 0

    lax.fori_loop(first, last, drain, 0)


def kernel(group, n_right, meta, panel, base, *refs):
    if group == len(GROUPS) - 2:
        total, token, out, right_panel, sems = refs[-5:]
        done = meta[TOFF + group]
        send_tiles(meta, total, out, sems, 0, done)
    else:
        total, token, right_panel = refs[-3:]
    token[...] = jnp.zeros_like(token)
    first = split_rows(refs[:n_right], right_panel)
    if group == 0:

        def own(at, _):
            right_panel[first + at, :BS] = panel[at, :, :BS]
            right_panel[first + at, BS:] = panel[at, :, BS:]
            return 0

        lax.fori_loop(0, NNZ, own, 0)
    add_pairs(group, meta, panel, right_panel, total)
    if group == len(GROUPS) - 2:
        wait_tiles(meta, total, out, sems, 0, done)


def last_kernel(group, n_right, meta, panel, base, *refs):
    out, right_panel, acc, sems = refs[-4:]
    before, t0, t1 = meta[TOFF + group - 1], meta[TOFF + group], meta[TOFF + group + 1]
    send_tiles(meta, base, out, sems, before, t0)

    def begin(i, _):
        tile = meta[TLIST + i] >> 8
        acc[tile] = base[tile]
        return 0

    lax.fori_loop(t0, t1, begin, 0)
    acc[OT] = jnp.zeros((BS, BS), jnp.float32)
    split_rows(refs[:n_right], right_panel)
    add_pairs(group, meta, panel, right_panel, acc)
    send_tiles(meta, acc, out, sems, t0, t1)
    wait_tiles(meta, base, out, sems, before, t0)
    wait_tiles(meta, acc, out, sems, t0, t1)


VMEM_SPEC = pl.BlockSpec(memory_space=pltpu.VMEM)
SMEM_SPEC = pl.BlockSpec(memory_space=pltpu.SMEM)
TOTAL = pltpu.VMEM((OT + 1, BS, BS), jnp.float32)
TOKEN = jax.ShapeDtypeStruct((8, BS), jnp.float32)
ANY_SPEC = pl.BlockSpec(memory_space=pl.ANY)


VMEM_SPEC = pl.BlockSpec(memory_space=pltpu.VMEM)
SMEM_SPEC = pl.BlockSpec(memory_space=pltpu.SMEM)
TOTAL = pltpu.VMEM((OT + 1, BS, BS), jnp.float32)
TOKEN = jax.ShapeDtypeStruct((8, BS), jnp.float32)
ANY_SPEC = pl.BlockSpec(memory_space=pl.ANY)


def in_hbm(block):
    return pltpu.with_memory_space_constraint(block, pltpu.HBM)


def run_prepare(meta, left):
    return pl.pallas_call(
        functools.partial(prepare, len(left)),
        out_shape=[
            pltpu.VMEM((len(left) * NNZ, BS, 2 * BS), jnp.bfloat16),
            TOTAL,
            TOKEN,
        ],
        in_specs=[SMEM_SPEC] + [VMEM_SPEC] * len(left),
        out_specs=[VMEM_SPEC, VMEM_SPEC, VMEM_SPEC],
        cost_estimate=pl.CostEstimate(
            flops=5 << 20, bytes_accessed=12 << 20, transcendentals=0
        ),
        compiler_params=pltpu.CompilerParams(vmem_limit_bytes=8 << 20),
        name="left_panel",
    )(meta, *left)


def run_group(group, meta, panel, base, right, order):
    last, begun = group == len(GROUPS) - 1, group == len(GROUPS) - 2
    whole = jax.ShapeDtypeStruct((OT, BS, BS), jnp.float32)
    scratch = [pltpu.VMEM((len(GROUPS[group]) * NNZ, 2 * BS, BS), jnp.bfloat16)]
    if last:
        scratch += [pltpu.VMEM((OT + 1, BS, BS), jnp.float32)]
    if last or begun:
        scratch += [pltpu.SemaphoreType.DMA((OT,))]
    return pl.pallas_call(
        functools.partial(last_kernel if last else kernel, group, len(right)),
        out_shape=whole if last else [TOTAL, TOKEN] + [whole] * begun,
        in_specs=[SMEM_SPEC] + [VMEM_SPEC] * (len(right) + 2) + [ANY_SPEC],
        out_specs=ANY_SPEC if last else [VMEM_SPEC, VMEM_SPEC] + [ANY_SPEC] * begun,
        scratch_shapes=scratch,
        input_output_aliases={len(right) + 3: 0} if last else {2: 0},
        cost_estimate=pl.CostEstimate(
            flops=len(GROUPS[group]) * NNZ * 16 * BS**3,
            bytes_accessed=4 << 20,
            transcendentals=0,
        ),
        compiler_params=pltpu.CompilerParams(vmem_limit_bytes=8 << 20),
        name=f"pairs_{group}",
    )(meta, panel, base, *right, order)


def shards(p_vals, p_cols, perm, out_pattern, branch_flag):
    row_index = lax.axis_index("row")
    col_index = lax.axis_index("col")
    meta, ids = work_list(row_index, col_index, perm, p_cols, out_pattern[0, 0], branch_flag[0, 0])

    one1 = ring(p_vals, 1)
    partner = swap_cores(p_vals)
    other1 = ring(after(p_vals, meta), -1)
    near = next_chip(after(p_vals, partner))
    near_partner = next_chip(partner)
    one2 = ring(one1, 1)
    near_swapped = swap_cores(after(near, one1))
    other2 = ring(after(other1, near_partner, meta), -1)
    far_partner = next_chip(near_partner)
    near_partner_swapped = swap_cores(near_partner)
    one2_low, one2_high = one2[:, :HALF], one2[:, HALF:]
    other2_low, other2_high = other2[:, :HALF], other2[:, HALF:]
    one3_low = ring(one2_low, 1)
    other3_high = ring(other2_high, -1)
    one3_high = ring(after(one2_high, other2), 1)
    other3_low = ring(after(other2_low, near_partner_swapped), -1)
    panel, base, token = run_prepare(
        meta,
        [
            p_vals,
            partner,
            near,
            near_partner,
            far_partner,
            near_swapped,
            near_partner_swapped,
        ],
    )
    before4, token = hold(one3_low, token)
    one4_low = ring(before4, 1)
    other4_high = ring(other3_high, -1)
    total, token = run_group(0, meta, panel, base, [one1, other1], token)
    total, token = run_group(1, meta, panel, total, [one2, other2], token)
    total, _, out = run_group(
        2, meta, panel, total, [one3_low, one3_high, other3_low, other3_high], token
    )
    out = run_group(3, meta, panel, total, [one4_low, other4_high], out)
    return out.reshape((1, 1) + out.shape)


def solution(mesh):
    return jax.shard_map(
        shards,
        mesh=mesh,
        in_specs=(
            P(("row", "col"), None, None, None),
            P(),
            P(),
            P("row", "col", None, None),
            P("row", "col"),
        ),
        out_specs=P("row", "col", None, None, None),
        check_vma=False,
    )
```

```python
import functools

import jax
import jax.numpy as jnp
from jax import lax
from jax.experimental import pallas as pl
from jax.experimental.pallas import tpu as pltpu
from jax.sharding import PartitionSpec as P

BS = 128
NNZ = 12
OT = 24
HALF = NNZ // 2
UNROLL = 4
LIST = 320
Z_EVEN = (-1, 1, 0, -2, 2, -3, 3, 4)
Z_ODD = (1, -1, 0, 2, -2, 3, -3, 4)
X_EVEN = (0, 1, -2, -1, -3, 3, 2)
X_ODD = (0, -1, 2, 1, 3, -3, -2)
GROUPS = ((0, 1, 2), (3, 4), (5, 6), (7,))
NT = (((1,), (1,)), ((), ()))
DUMMY = OT << 16
TLIST = LIST
POFF = TLIST + 32
TOFF = POFF + 8
FLAG = TOFF + 8
META = 384


def swap_cores(block):
    n = lax.axis_size("col")
    return lax.ppermute(block, "col", [(i, i ^ 1) for i in range(n)])


def next_chip(block):
    n = lax.axis_size("col")
    return lax.ppermute(block, "col", [(i, (i + (-2 if i % 2 else 2)) % n) for i in range(n)])


def ring(block, turn):
    rows, cols = lax.axis_size("row"), lax.axis_size("col")
    route = []
    for r in range(rows):
        for c in range(cols):
            step = turn if c % 2 == 0 else -turn
            route.append((r * cols + c, (r + step) % rows * cols + c))
    return lax.ppermute(block, ("row", "col"), route)


def after(block, *others):
    return lax.optimization_barrier((block, others))[0]


def hold(block, token):
    return lax.optimization_barrier((block, token))


def pick(onehot, table):
    return jnp.dot(onehot.astype(jnp.int32), table, preferred_element_type=jnp.int32)


def work_list(row_index, col_index, perm, p_cols, out_pairs, flag):
    n_rows, n_cols = lax.axis_size("row"), lax.axis_size("col")
    even = (col_index % 2) == 0
    steps = jnp.where(even, jnp.array(X_EVEN, jnp.int32), jnp.array(X_ODD, jnp.int32))
    left_pos = row_index * n_cols + jnp.mod(col_index + steps, n_cols)
    turns = jnp.where(even, jnp.array(Z_EVEN, jnp.int32), jnp.array(Z_ODD, jnp.int32))
    right_pos = jnp.mod(row_index + turns, n_rows) * n_cols + col_index
    pos = jnp.concatenate([left_pos, right_pos])
    onehot = pos[:, None] == jnp.arange(perm.shape[0], dtype=jnp.int32)[None, :]
    ids = jnp.sum(jnp.where(onehot, perm[None, :], 0), axis=1)
    cols = pick(onehot, p_cols)
    nl = len(X_EVEN)
    left_hot = out_pairs[:, 0:1] == ids[None, :nl]
    right_hot = out_pairs[:, 1:2] == ids[None, nl:]
    left_cols = pick(left_hot, cols[:nl])
    right_cols = pick(right_hot, cols[nl:])
    left_at = jnp.sum(jnp.where(left_hot, jnp.arange(nl, dtype=jnp.int32)[None, :], 0), axis=1)
    right_at = jnp.sum(
        jnp.where(right_hot, jnp.arange(len(Z_EVEN), dtype=jnp.int32)[None, :], 0), axis=1
    )
    group_of = [g for row in range(len(Z_EVEN)) for g, rows in enumerate(GROUPS) if row in rows]
    group = jnp.sum(jnp.where(right_hot, jnp.array(group_of, jnp.int32)[None, :], 0), axis=1)
    slots = jnp.arange(NNZ, dtype=jnp.int32)
    match = left_cols[:, :, None] == right_cols[:, None, :]
    present = jnp.any(match, axis=2)
    partner = jnp.sum(jnp.where(match, slots[None, None, :], 0), axis=2)
    tiles = jnp.arange(OT, dtype=jnp.int32)
    payload = (
        (tiles[:, None] << 16)
        + ((left_at[:, None] * NNZ + slots[None, :]) << 8)
        + right_at[:, None] * NNZ
        + partner
    )
    count = jnp.sum(present.astype(jnp.int32), axis=1)
    earlier = (group[:, None] == group[None, :]) & (tiles[None, :] < tiles[:, None])
    row_start = jnp.sum(jnp.where(earlier, count[None, :], 0), axis=1)
    gs = jnp.arange(8, dtype=jnp.int32)
    in_group = group[None, :] == gs[:, None]
    steps_of = (jnp.sum(jnp.where(in_group, count[None, :], 0), axis=1) + UNROLL - 1) // UNROLL
    before = gs[None, :] < gs[:, None]
    step_start = jnp.sum(jnp.where(before, steps_of[None, :], 0), axis=1)
    tile_start = jnp.sum((group[None, :] < gs[:, None]).astype(jnp.int32), axis=1)
    ahead = jnp.sum(
        (present[:, None, :] & (slots[None, None, :] < slots[None, :, None])).astype(jnp.int32),
        axis=2,
    )
    group_start = jnp.sum(jnp.where(in_group, step_start[:, None], 0), axis=0) * UNROLL
    rank = jnp.where(present, group_start[:, None] + row_start[:, None] + ahead, -1)
    places = jnp.arange(LIST, dtype=jnp.int32)
    pairs = DUMMY + jnp.sum(
        jnp.where(rank[:, :, None] == places[None, None, :], payload[:, :, None] - DUMMY, 0),
        axis=(0, 1),
    )
    own_hit = left_cols == out_pairs[:, 1:2]
    own = jnp.sum(
        jnp.where(own_hit, left_at[:, None] * NNZ + slots[None, :] + 1, 0), axis=1
    )
    tile_rank = jnp.sum(
        ((group[None, :] < group[:, None]) | earlier).astype(jnp.int32), axis=1
    )
    tile_list = jnp.sum(
        jnp.where(
            tile_rank[:, None] == jnp.arange(32, dtype=jnp.int32)[None, :],
            ((tiles << 8) + own)[:, None],
            0,
        ),
        axis=0,
    )
    tail = jnp.full((META - FLAG,), flag, jnp.int32)
    return jnp.concatenate([pairs, tile_list, step_start, tile_start, tail]), ids


def split(block):
    high = block.astype(jnp.bfloat16)
    return high, (block - high.astype(jnp.float32)).astype(jnp.bfloat16)


def prepare(n_left, meta, *refs):
    left = refs[:n_left]
    panel, base, token = refs[n_left:]
    token[...] = jnp.zeros_like(token)
    use = meta[FLAG] == 1

    def clear(tile, _):
        base[tile] = jnp.zeros((BS, BS), jnp.float32)
        return 0

    lax.fori_loop(0, OT + 1, clear, 0)
    for row, ref in enumerate(left):

        def block(at, _, row=row, ref=ref):
            high, low = split(ref[0, at])
            panel[row * NNZ + at, :, :BS] = high
            panel[row * NNZ + at, :, BS:] = low
            return 0

        lax.fori_loop(0, NNZ, block, 0)

    @pl.when(use)
    def _():
        def own(i, _):
            item = meta[TLIST + i]
            tile, at = item >> 8, (item & 255) - 1
            for row, ref in enumerate(left):

                @pl.when((at >= row * NNZ) & (at < (row + 1) * NNZ))
                def _(row=row, ref=ref):
                    base[tile] = 2.0 * ref[0, at - row * NNZ]

            return 0

        lax.fori_loop(0, OT, own, 0)


def split_rows(right, right_panel):
    first = 0
    for ref in right:
        split_row(ref.at[0], first, ref.shape[1], right_panel)
        first += ref.shape[1]
    return first


def split_row(blocks, first, size, right_panel):
    def block(at, _):
        high, low = split(blocks[at])
        right_panel[first + at, :BS] = high
        right_panel[first + at, BS:] = low
        return 0

    lax.fori_loop(0, size, block, 0)


def add_pairs(group, meta, panel, right_panel, acc):
    first = GROUPS[group][0] * NNZ
    sign = jnp.where(meta[FLAG] == 1, -1.0, 1.0)

    def some(at, count):
        for k in range(count):
            item = meta[at + k]
            tile = item >> 16
            l_at = (item >> 8) & 255
            r_at = jnp.maximum((item & 255) - first, 0)
            r = right_panel[r_at]
            both = lax.dot_general(
                panel[l_at],
                jnp.concatenate([r, r], axis=1),
                NT,
                preferred_element_type=jnp.float32,
            )
            acc[tile] = acc[tile] + sign * (both[:, :BS] + both[:, BS:])

    start, end = meta[POFF + group], meta[POFF + group + 1]

    def pairs(step, _):
        some((start + 2 * step) * UNROLL, 2 * UNROLL)
        return 0

    lax.fori_loop(0, (end - start) // 2, pairs, 0)

    @pl.when((end - start) % 2 == 1)
    def _():
        some((end - 1) * UNROLL, UNROLL)


def tile_copy(meta, source, out, sems, i):
    tile = meta[TLIST + i] >> 8
    return pltpu.make_async_copy(source.at[tile], out.at[tile], sems.at[tile])


def send_tiles(meta, source, out, sems, first, last):
    def leave(i, _):
        tile_copy(meta, source, out, sems, i).start()
        return 0

    lax.fori_loop(first, last, leave, 0)


def wait_tiles(meta, source, out, sems, first, last):
    def drain(i, _):
        tile_copy(meta, source, out, sems, i).wait()
        return 0

    lax.fori_loop(first, last, drain, 0)


def kernel(group, n_right, meta, panel, base, *refs):
    if group == len(GROUPS) - 2:
        total, token, out, right_panel, sems = refs[-5:]
        done = meta[TOFF + group]
        send_tiles(meta, total, out, sems, 0, done)
    else:
        total, token, right_panel = refs[-3:]
    token[...] = jnp.zeros_like(token)
    first = split_rows(refs[:n_right], right_panel)
    if group == 0:

        def own(at, _):
            right_panel[first + at, :BS] = panel[at, :, :BS]
            right_panel[first + at, BS:] = panel[at, :, BS:]
            return 0

        lax.fori_loop(0, NNZ, own, 0)
    add_pairs(group, meta, panel, right_panel, total)
    if group == len(GROUPS) - 2:
        wait_tiles(meta, total, out, sems, 0, done)


def last_kernel(group, n_right, meta, panel, base, *refs):
    out, right_panel, acc, sems = refs[-4:]
    before, t0, t1 = meta[TOFF + group - 1], meta[TOFF + group], meta[TOFF + group + 1]
    send_tiles(meta, base, out, sems, before, t0)

    def begin(i, _):
        tile = meta[TLIST + i] >> 8
        acc[tile] = base[tile]
        return 0

    lax.fori_loop(t0, t1, begin, 0)
    acc[OT] = jnp.zeros((BS, BS), jnp.float32)
    split_rows(refs[:n_right], right_panel)
    add_pairs(group, meta, panel, right_panel, acc)
    send_tiles(meta, acc, out, sems, t0, t1)
    wait_tiles(meta, base, out, sems, before, t0)
    wait_tiles(meta, acc, out, sems, t0, t1)


VMEM_SPEC = pl.BlockSpec(memory_space=pltpu.VMEM)
SMEM_SPEC = pl.BlockSpec(memory_space=pltpu.SMEM)
TOTAL = pltpu.VMEM((OT + 1, BS, BS), jnp.float32)
TOKEN = jax.ShapeDtypeStruct((8, BS), jnp.float32)
ANY_SPEC = pl.BlockSpec(memory_space=pl.ANY)


VMEM_SPEC = pl.BlockSpec(memory_space=pltpu.VMEM)
SMEM_SPEC = pl.BlockSpec(memory_space=pltpu.SMEM)
TOTAL = pltpu.VMEM((OT + 1, BS, BS), jnp.float32)
TOKEN = jax.ShapeDtypeStruct((8, BS), jnp.float32)
ANY_SPEC = pl.BlockSpec(memory_space=pl.ANY)


def in_hbm(block):
    return pltpu.with_memory_space_constraint(block, pltpu.HBM)


def run_prepare(meta, left):
    return pl.pallas_call(
        functools.partial(prepare, len(left)),
        out_shape=[
            pltpu.VMEM((len(left) * NNZ, BS, 2 * BS), jnp.bfloat16),
            TOTAL,
            TOKEN,
        ],
        in_specs=[SMEM_SPEC] + [VMEM_SPEC] * len(left),
        out_specs=[VMEM_SPEC, VMEM_SPEC, VMEM_SPEC],
        cost_estimate=pl.CostEstimate(
            flops=5 << 20, bytes_accessed=12 << 20, transcendentals=0
        ),
        compiler_params=pltpu.CompilerParams(vmem_limit_bytes=8 << 20),
        name="left_panel",
    )(meta, *left)


def run_group(group, meta, panel, base, right, order):
    last, begun = group == len(GROUPS) - 1, group == len(GROUPS) - 2
    whole = jax.ShapeDtypeStruct((OT, BS, BS), jnp.float32)
    scratch = [pltpu.VMEM((len(GROUPS[group]) * NNZ, 2 * BS, BS), jnp.bfloat16)]
    if last:
        scratch += [pltpu.VMEM((OT + 1, BS, BS), jnp.float32)]
    if last or begun:
        scratch += [pltpu.SemaphoreType.DMA((OT,))]
    return pl.pallas_call(
        functools.partial(last_kernel if last else kernel, group, len(right)),
        out_shape=whole if last else [TOTAL, TOKEN] + [whole] * begun,
        in_specs=[SMEM_SPEC] + [VMEM_SPEC] * (len(right) + 2) + [ANY_SPEC],
        out_specs=ANY_SPEC if last else [VMEM_SPEC, VMEM_SPEC] + [ANY_SPEC] * begun,
        scratch_shapes=scratch,
        input_output_aliases={len(right) + 3: 0} if last else {2: 0},
        cost_estimate=pl.CostEstimate(
            flops=len(GROUPS[group]) * NNZ * 16 * BS**3,
            bytes_accessed=4 << 20,
            transcendentals=0,
        ),
        compiler_params=pltpu.CompilerParams(vmem_limit_bytes=8 << 20),
        name=f"pairs_{group}",
    )(meta, panel, base, *right, order)


def shards(p_vals, p_cols, perm, out_pattern, branch_flag):
    row_index = lax.axis_index("row")
    col_index = lax.axis_index("col")
    meta, ids = work_list(row_index, col_index, perm, p_cols, out_pattern[0, 0], branch_flag[0, 0])

    one1 = ring(p_vals, 1)
    partner = swap_cores(p_vals)
    other1 = ring(after(p_vals, meta), -1)
    near = next_chip(after(p_vals, partner))
    near_partner = next_chip(partner)
    one2 = ring(one1, 1)
    near_swapped = swap_cores(after(near, one2))
    other2 = ring(after(other1, near_partner, meta), -1)
    far_partner = next_chip(near_partner)
    near_partner_swapped = swap_cores(near_partner)
    one2_low, one2_high = one2[:, :HALF], one2[:, HALF:]
    other2_low, other2_high = other2[:, :HALF], other2[:, HALF:]
    one3_low = ring(one2_low, 1)
    other3_high = ring(other2_high, -1)
    one3_high = ring(after(one2_high, other2), 1)
    other3_low = ring(after(other2_low, near_partner_swapped), -1)
    panel, base, token = run_prepare(
        meta,
        [
            p_vals,
            partner,
            near,
            near_partner,
            far_partner,
            near_swapped,
            near_partner_swapped,
        ],
    )
    before4, token = hold(one3_low, token)
    one4_low = ring(before4, 1)
    other4_high = ring(other3_high, -1)
    total, token = run_group(0, meta, panel, base, [one1, other1], token)
    total, token = run_group(1, meta, panel, total, [one2, other2], token)
    total, _, out = run_group(
        2, meta, panel, total, [one3_low, one3_high, other3_low, other3_high], token
    )
    out = run_group(3, meta, panel, total, [one4_low, other4_high], out)
    return out.reshape((1, 1) + out.shape)


def solution(mesh):
    return jax.shard_map(
        shards,
        mesh=mesh,
        in_specs=(
            P(("row", "col"), None, None, None),
            P(),
            P(),
            P("row", "col", None, None),
            P("row", "col"),
        ),
        out_specs=P("row", "col", None, None, None),
        check_vma=False,
    )
```

```python
import functools

import jax
import jax.numpy as jnp
from jax import lax
from jax.experimental import pallas as pl
from jax.experimental.pallas import tpu as pltpu
from jax.sharding import PartitionSpec as P

BS = 128
NNZ = 12
OT = 24
HALF = NNZ // 2
UNROLL = 4
LIST = 320
Z_EVEN = (-1, 1, 0, -2, 2, -3, 3, 4)
Z_ODD = (1, -1, 0, 2, -2, 3, -3, 4)
X_EVEN = (0, 1, -2, -1, -3, 3, 2)
X_ODD = (0, -1, 2, 1, 3, -3, -2)
GROUPS = ((0, 1, 2), (3, 4), (5, 6), (7,))
NT = (((1,), (1,)), ((), ()))
DUMMY = OT << 16
TLIST = LIST
POFF = TLIST + 32
TOFF = POFF + 8
FLAG = TOFF + 8
META = 384


def swap_cores(block):
    n = lax.axis_size("col")
    return lax.ppermute(block, "col", [(i, i ^ 1) for i in range(n)])


def next_chip(block):
    n = lax.axis_size("col")
    return lax.ppermute(block, "col", [(i, (i + (-2 if i % 2 else 2)) % n) for i in range(n)])


def ring(block, turn):
    rows, cols = lax.axis_size("row"), lax.axis_size("col")
    route = []
    for r in range(rows):
        for c in range(cols):
            step = turn if c % 2 == 0 else -turn
            route.append((r * cols + c, (r + step) % rows * cols + c))
    return lax.ppermute(block, ("row", "col"), route)


def after(block, *others):
    return lax.optimization_barrier((block, others))[0]


def hold(block, token):
    return lax.optimization_barrier((block, token))


def pick(onehot, table):
    return jnp.dot(onehot.astype(jnp.int32), table, preferred_element_type=jnp.int32)


def work_list(row_index, col_index, perm, p_cols, out_pairs, flag):
    n_rows, n_cols = lax.axis_size("row"), lax.axis_size("col")
    even = (col_index % 2) == 0
    steps = jnp.where(even, jnp.array(X_EVEN, jnp.int32), jnp.array(X_ODD, jnp.int32))
    left_pos = row_index * n_cols + jnp.mod(col_index + steps, n_cols)
    turns = jnp.where(even, jnp.array(Z_EVEN, jnp.int32), jnp.array(Z_ODD, jnp.int32))
    right_pos = jnp.mod(row_index + turns, n_rows) * n_cols + col_index
    pos = jnp.concatenate([left_pos, right_pos])
    onehot = pos[:, None] == jnp.arange(perm.shape[0], dtype=jnp.int32)[None, :]
    ids = jnp.sum(jnp.where(onehot, perm[None, :], 0), axis=1)
    cols = pick(onehot, p_cols)
    nl = len(X_EVEN)
    left_hot = out_pairs[:, 0:1] == ids[None, :nl]
    right_hot = out_pairs[:, 1:2] == ids[None, nl:]
    left_cols = pick(left_hot, cols[:nl])
    right_cols = pick(right_hot, cols[nl:])
    left_at = jnp.sum(jnp.where(left_hot, jnp.arange(nl, dtype=jnp.int32)[None, :], 0), axis=1)
    right_at = jnp.sum(
        jnp.where(right_hot, jnp.arange(len(Z_EVEN), dtype=jnp.int32)[None, :], 0), axis=1
    )
    group_of = [g for row in range(len(Z_EVEN)) for g, rows in enumerate(GROUPS) if row in rows]
    group = jnp.sum(jnp.where(right_hot, jnp.array(group_of, jnp.int32)[None, :], 0), axis=1)
    slots = jnp.arange(NNZ, dtype=jnp.int32)
    match = left_cols[:, :, None] == right_cols[:, None, :]
    present = jnp.any(match, axis=2)
    partner = jnp.sum(jnp.where(match, slots[None, None, :], 0), axis=2)
    tiles = jnp.arange(OT, dtype=jnp.int32)
    payload = (
        (tiles[:, None] << 16)
        + ((left_at[:, None] * NNZ + slots[None, :]) << 8)
        + right_at[:, None] * NNZ
        + partner
    )
    count = jnp.sum(present.astype(jnp.int32), axis=1)
    earlier = (group[:, None] == group[None, :]) & (tiles[None, :] < tiles[:, None])
    row_start = jnp.sum(jnp.where(earlier, count[None, :], 0), axis=1)
    gs = jnp.arange(8, dtype=jnp.int32)
    in_group = group[None, :] == gs[:, None]
    steps_of = (jnp.sum(jnp.where(in_group, count[None, :], 0), axis=1) + UNROLL - 1) // UNROLL
    before = gs[None, :] < gs[:, None]
    step_start = jnp.sum(jnp.where(before, steps_of[None, :], 0), axis=1)
    tile_start = jnp.sum((group[None, :] < gs[:, None]).astype(jnp.int32), axis=1)
    ahead = jnp.sum(
        (present[:, None, :] & (slots[None, None, :] < slots[None, :, None])).astype(jnp.int32),
        axis=2,
    )
    group_start = jnp.sum(jnp.where(in_group, step_start[:, None], 0), axis=0) * UNROLL
    rank = jnp.where(present, group_start[:, None] + row_start[:, None] + ahead, -1)
    places = jnp.arange(LIST, dtype=jnp.int32)
    pairs = DUMMY + jnp.sum(
        jnp.where(rank[:, :, None] == places[None, None, :], payload[:, :, None] - DUMMY, 0),
        axis=(0, 1),
    )
    own_hit = left_cols == out_pairs[:, 1:2]
    own = jnp.sum(
        jnp.where(own_hit, left_at[:, None] * NNZ + slots[None, :] + 1, 0), axis=1
    )
    tile_rank = jnp.sum(
        ((group[None, :] < group[:, None]) | earlier).astype(jnp.int32), axis=1
    )
    tile_list = jnp.sum(
        jnp.where(
            tile_rank[:, None] == jnp.arange(32, dtype=jnp.int32)[None, :],
            ((tiles << 8) + own)[:, None],
            0,
        ),
        axis=0,
    )
    tail = jnp.full((META - FLAG,), flag, jnp.int32)
    return jnp.concatenate([pairs, tile_list, step_start, tile_start, tail]), ids


def split(block):
    high = block.astype(jnp.bfloat16)
    return high, (block - high.astype(jnp.float32)).astype(jnp.bfloat16)


def prepare(n_left, meta, *refs):
    left = refs[:n_left]
    panel, base, token = refs[n_left:]
    token[...] = jnp.zeros_like(token)
    use = meta[FLAG] == 1

    def clear(tile, _):
        base[tile] = jnp.zeros((BS, BS), jnp.float32)
        return 0

    lax.fori_loop(0, OT + 1, clear, 0)
    for row, ref in enumerate(left):

        def block(at, _, row=row, ref=ref):
            high, low = split(ref[0, at])
            panel[row * NNZ + at, :, :BS] = high
            panel[row * NNZ + at, :, BS:] = low
            return 0

        lax.fori_loop(0, NNZ, block, 0)

    @pl.when(use)
    def _():
        def own(i, _):
            item = meta[TLIST + i]
            tile, at = item >> 8, (item & 255) - 1

            @pl.when(at >= 0)
            def _():
                for row, ref in enumerate(left):

                    @pl.when((at >= row * NNZ) & (at < (row + 1) * NNZ))
                    def _(row=row, ref=ref):
                        base[tile] = 2.0 * ref[0, at - row * NNZ]

            return 0

        lax.fori_loop(0, OT, own, 0)


def split_rows(right, right_panel):
    first = 0
    for ref in right:
        split_row(ref.at[0], first, ref.shape[1], right_panel)
        first += ref.shape[1]
    return first


def split_row(blocks, first, size, right_panel):
    def block(at, _):
        high, low = split(blocks[at])
        right_panel[first + at, :BS] = high
        right_panel[first + at, BS:] = low
        return 0

    lax.fori_loop(0, size, block, 0)


def add_pairs(group, meta, panel, right_panel, acc):
    first = GROUPS[group][0] * NNZ
    sign = jnp.where(meta[FLAG] == 1, -1.0, 1.0)

    def some(at, count):
        for k in range(count):
            item = meta[at + k]
            tile = item >> 16
            l_at = (item >> 8) & 255
            r_at = jnp.maximum((item & 255) - first, 0)
            r = right_panel[r_at]
            both = lax.dot_general(
                panel[l_at],
                jnp.concatenate([r, r], axis=1),
                NT,
                preferred_element_type=jnp.float32,
            )
            acc[tile] = acc[tile] + sign * (both[:, :BS] + both[:, BS:])

    start, end = meta[POFF + group], meta[POFF + group + 1]

    def pairs(step, _):
        some((start + 2 * step) * UNROLL, 2 * UNROLL)
        return 0

    lax.fori_loop(0, (end - start) // 2, pairs, 0)

    @pl.when((end - start) % 2 == 1)
    def _():
        some((end - 1) * UNROLL, UNROLL)


def tile_copy(meta, source, out, sems, i):
    tile = meta[TLIST + i] >> 8
    return pltpu.make_async_copy(source.at[tile], out.at[tile], sems.at[tile])


def send_tiles(meta, source, out, sems, first, last):
    def leave(i, _):
        tile_copy(meta, source, out, sems, i).start()
        return 0

    lax.fori_loop(first, last, leave, 0)


def wait_tiles(meta, source, out, sems, first, last):
    def drain(i, _):
        tile_copy(meta, source, out, sems, i).wait()
        return 0

    lax.fori_loop(first, last, drain, 0)


def kernel(group, n_right, meta, panel, base, *refs):
    if group == len(GROUPS) - 2:
        total, token, out, right_panel, sems = refs[-5:]
        done = meta[TOFF + group]
        send_tiles(meta, total, out, sems, 0, done)
    else:
        total, token, right_panel = refs[-3:]
    token[...] = jnp.zeros_like(token)
    first = split_rows(refs[:n_right], right_panel)
    if group == 0:

        def own(at, _):
            right_panel[first + at, :BS] = panel[at, :, :BS]
            right_panel[first + at, BS:] = panel[at, :, BS:]
            return 0

        lax.fori_loop(0, NNZ, own, 0)
    add_pairs(group, meta, panel, right_panel, total)
    if group == len(GROUPS) - 2:
        wait_tiles(meta, total, out, sems, 0, done)


def last_kernel(group, n_right, meta, panel, base, *refs):
    out, right_panel, acc, sems = refs[-4:]
    before, t0, t1 = meta[TOFF + group - 1], meta[TOFF + group], meta[TOFF + group + 1]
    send_tiles(meta, base, out, sems, before, t0)

    def begin(i, _):
        tile = meta[TLIST + i] >> 8
        acc[tile] = base[tile]
        return 0

    lax.fori_loop(t0, t1, begin, 0)
    acc[OT] = jnp.zeros((BS, BS), jnp.float32)
    split_rows(refs[:n_right], right_panel)
    add_pairs(group, meta, panel, right_panel, acc)
    send_tiles(meta, acc, out, sems, t0, t1)
    wait_tiles(meta, base, out, sems, before, t0)
    wait_tiles(meta, acc, out, sems, t0, t1)


VMEM_SPEC = pl.BlockSpec(memory_space=pltpu.VMEM)
SMEM_SPEC = pl.BlockSpec(memory_space=pltpu.SMEM)
TOTAL = pltpu.VMEM((OT + 1, BS, BS), jnp.float32)
TOKEN = jax.ShapeDtypeStruct((8, BS), jnp.float32)
ANY_SPEC = pl.BlockSpec(memory_space=pl.ANY)


VMEM_SPEC = pl.BlockSpec(memory_space=pltpu.VMEM)
SMEM_SPEC = pl.BlockSpec(memory_space=pltpu.SMEM)
TOTAL = pltpu.VMEM((OT + 1, BS, BS), jnp.float32)
TOKEN = jax.ShapeDtypeStruct((8, BS), jnp.float32)
ANY_SPEC = pl.BlockSpec(memory_space=pl.ANY)


def in_hbm(block):
    return pltpu.with_memory_space_constraint(block, pltpu.HBM)


def run_prepare(meta, left):
    return pl.pallas_call(
        functools.partial(prepare, len(left)),
        out_shape=[
            pltpu.VMEM((len(left) * NNZ, BS, 2 * BS), jnp.bfloat16),
            TOTAL,
            TOKEN,
        ],
        in_specs=[SMEM_SPEC] + [VMEM_SPEC] * len(left),
        out_specs=[VMEM_SPEC, VMEM_SPEC, VMEM_SPEC],
        cost_estimate=pl.CostEstimate(
            flops=5 << 20, bytes_accessed=12 << 20, transcendentals=0
        ),
        compiler_params=pltpu.CompilerParams(vmem_limit_bytes=8 << 20),
        name="left_panel",
    )(meta, *left)


def run_group(group, meta, panel, base, right, order):
    last, begun = group == len(GROUPS) - 1, group == len(GROUPS) - 2
    whole = jax.ShapeDtypeStruct((OT, BS, BS), jnp.float32)
    scratch = [pltpu.VMEM((len(GROUPS[group]) * NNZ, 2 * BS, BS), jnp.bfloat16)]
    if last:
        scratch += [pltpu.VMEM((OT + 1, BS, BS), jnp.float32)]
    if last or begun:
        scratch += [pltpu.SemaphoreType.DMA((OT,))]
    return pl.pallas_call(
        functools.partial(last_kernel if last else kernel, group, len(right)),
        out_shape=whole if last else [TOTAL, TOKEN] + [whole] * begun,
        in_specs=[SMEM_SPEC] + [VMEM_SPEC] * (len(right) + 2) + [ANY_SPEC],
        out_specs=ANY_SPEC if last else [VMEM_SPEC, VMEM_SPEC] + [ANY_SPEC] * begun,
        scratch_shapes=scratch,
        input_output_aliases={len(right) + 3: 0} if last else {2: 0},
        cost_estimate=pl.CostEstimate(
            flops=len(GROUPS[group]) * NNZ * 16 * BS**3,
            bytes_accessed=4 << 20,
            transcendentals=0,
        ),
        compiler_params=pltpu.CompilerParams(vmem_limit_bytes=8 << 20),
        name=f"pairs_{group}",
    )(meta, panel, base, *right, order)


def shards(p_vals, p_cols, perm, out_pattern, branch_flag):
    row_index = lax.axis_index("row")
    col_index = lax.axis_index("col")
    meta, ids = work_list(row_index, col_index, perm, p_cols, out_pattern[0, 0], branch_flag[0, 0])

    one1 = ring(p_vals, 1)
    partner = swap_cores(p_vals)
    other1 = ring(after(p_vals, meta), -1)
    near = next_chip(after(p_vals, partner))
    near_partner = next_chip(partner)
    one2 = ring(one1, 1)
    near_swapped = swap_cores(after(near, one2))
    other2 = ring(after(other1, near_partner, meta), -1)
    far_partner = next_chip(near_partner)
    near_partner_swapped = swap_cores(near_partner)
    one2_low, one2_high = one2[:, :HALF], one2[:, HALF:]
    other2_low, other2_high = other2[:, :HALF], other2[:, HALF:]
    one3_low = ring(one2_low, 1)
    other3_high = ring(other2_high, -1)
    one3_high = ring(after(one2_high, other2), 1)
    other3_low = ring(after(other2_low, near_partner_swapped), -1)
    panel, base, token = run_prepare(
        meta,
        [
            p_vals,
            partner,
            near,
            near_partner,
            far_partner,
            near_swapped,
            near_partner_swapped,
        ],
    )
    before4, token = hold(one3_low, token)
    one4_low = ring(before4, 1)
    other4_high = ring(other3_high, -1)
    total, token = run_group(0, meta, panel, base, [one1, other1], token)
    total, token = run_group(1, meta, panel, total, [one2, other2], token)
    total, _, out = run_group(
        2, meta, panel, total, [one3_low, one3_high, other3_low, other3_high], token
    )
    out = run_group(3, meta, panel, total, [one4_low, other4_high], out)
    return out.reshape((1, 1) + out.shape)


def solution(mesh):
    return jax.shard_map(
        shards,
        mesh=mesh,
        in_specs=(
            P(("row", "col"), None, None, None),
            P(),
            P(),
            P("row", "col", None, None),
            P("row", "col"),
        ),
        out_specs=P("row", "col", None, None, None),
        check_vma=False,
    )
```
